32 devices in a mesh: ctx: 8 (over y, x, core), tp: 4 (over z).
Axes of the slice: x: 2, y: 2, z: 4, core: 2. Of those that a mesh axis runs over, the one named last changes fastest.
Arguments:
- queries: bfloat16 [1, 8192, 4096], P(None, 'ctx', 'tp'), may hold values from -6 to 6
- keys: bfloat16 [1, 8192, 1024], P(None, 'ctx', 'tp'), may hold values from -6 to 6
- values: bfloat16 [1, 8192, 1024], P(None, 'ctx', 'tp'), may hold values from -6 to 6
- gates: int32 [1, 16, 8, 3], P(None, 'ctx', 'tp'), may hold values from 0 to 15, as said below
- out_weight: bfloat16 [4096, 4096], P('tp'), may hold values from -0.09375 to 0.09375
Outputs:
- projected: bfloat16 [1, 8192, 4096], P(None, 'ctx', 'tp')
The draws below stay inside these ranges and needn't reach their ends.
Inputs may be any that keep to these rules, and one draw needn't show every extreme that they name: `gates`: for each sequence and key-value head, the 6 entries of query blocks 2 c to 2 c + 1 name blocks of 6 different values of (block // 2).
All inputs are finite; a program needn't handle non-finite values.
Results may differ from the reference program's by a relative error of at most 0.015.
Values may be sent and summed in bfloat16 or wider, within the bound.
A program may use at most 128 MiB of HBM per device.

```python
import jax
import jax.numpy as jnp
from jax import lax

HQ = 32
KVH = 8
HD = 128
D_OUT = 4096
TOKB = 512
PICKS = 3
QB_DEV = 2
SEQ = 1
NB = 16
L = 8192
N_TP = 4


def draw_queries(key, part):
    drawn = jax.random.truncated_normal(jax.random.fold_in(key, 11), -6.0, 6.0, (SEQ, L, HQ * HD), jnp.float32)
    return drawn.astype(jnp.bfloat16)


def draw_keys(key, part):
    drawn = jax.random.truncated_normal(jax.random.fold_in(key, 13), -6.0, 6.0, (SEQ, L, KVH * HD), jnp.float32)
    return drawn.astype(jnp.bfloat16)


def draw_gates(key, part):
    device_count = NB // QB_DEV
    pick_total = PICKS * QB_DEV
    random_scores = jax.random.randint(jax.random.fold_in(key, 21), (SEQ, device_count, KVH, device_count), 0, 2 ** 17)
    column = jnp.arange(device_count, dtype=jnp.int32)
    row_of = column[None, :, None, None]
    col_of = column[None, None, None, :]
    ranked = random_scores * 4096 + col_of
    forced = (row_of == 0) & (col_of == device_count - 1) | (row_of == device_count - 1) & (col_of == 0)
    ranked = jnp.where(forced, ranked + 2 ** 30, ranked)
    reachable = jnp.where(column == 0, device_count, jnp.maximum(column, pick_total))
    allowed = col_of < reachable[None, :, None, None]
    ranked = jnp.where(allowed, ranked, -1 - col_of)
    chosen = lax.top_k(ranked, pick_total)[1].astype(jnp.int32)
    offsets = jax.random.randint(jax.random.fold_in(key, 23), chosen.shape, 0, QB_DEV)
    row_pick = jnp.broadcast_to(column[None, :, None, None], chosen.shape)
    offsets = jnp.where((row_pick == 0) & (chosen == device_count - 1), QB_DEV - 1, offsets)
    offsets = jnp.where((row_pick == device_count - 1) & (chosen == 0), 0, offsets)
    picked = (chosen * QB_DEV + offsets).astype(jnp.int32)
    picked = picked.reshape(SEQ, device_count, KVH, QB_DEV, PICKS)
    return jnp.transpose(picked, (0, 1, 3, 2, 4)).reshape(SEQ, NB, KVH, PICKS)


def block_scale(stream_key, extent, shards, smallest, high):
    def one(dim, blocks):
        heights = jax.random.uniform(jax.random.fold_in(jax.random.fold_in(stream_key, 6), dim), (blocks,), jnp.float32, smallest / len(shards), high / len(shards))
        return jnp.repeat(jnp.exp(heights), extent[dim] // blocks).reshape((-1,) + (1,) * (len(extent) - dim - 1))

    loudness = one(*shards[0])
    for cut in shards[1:]:
        loudness = loudness * one(*cut)
    return loudness


def centred(stream_key, extent, width, most, split=(), held_as=jnp.bfloat16):
    result = jax.random.normal(stream_key, extent, jnp.float32) * width
    if len(split) > 0:
        result = block_scale(stream_key, extent, split, -0.22, 0.18) * result
    return jnp.clip(result, min=-most, max=most).astype(held_as)


def setup_inputs(seed: int = 0) -> dict:
    key_list = jax.random.split(jax.random.key(seed), 6)
    queries = draw_queries(jax.random.fold_in(key_list[5], 71), 0)
    keys = draw_keys(jax.random.fold_in(key_list[5], 71), 0)
    values = centred(key_list[2], (SEQ, L, KVH * HD), 1.0, 6.0, ((1, 8), (2, 4)))
    gates = draw_gates(jax.random.fold_in(key_list[5], 71), 0)
    out_weight = centred(key_list[4], (HQ * HD, D_OUT), (HQ * HD) ** -0.5, 0.09375, ((0, 4),))
    return {"queries": queries, "keys": keys, "values": values, "gates": gates, "out_weight": out_weight}


def attend_rows(query_block, key_rows, value_rows, allowed):
    score_scale = HD ** -0.5
    scores = jnp.einsum("qhgd,hkd->hgqk", query_block.astype(jnp.float32), key_rows.astype(jnp.float32)) * score_scale
    scores = jnp.where(allowed[:, None], scores, -jnp.inf)
    largest = jnp.max(scores, axis=-1, keepdims=True)
    raw_weights = jnp.exp(scores - largest)
    denominator = jnp.sum(raw_weights, axis=-1)
    weights = raw_weights.astype(jnp.bfloat16)
    weighted = jnp.einsum("hgqk,hkd->qhgd", weights.astype(jnp.float32), value_rows.astype(jnp.float32))
    weighted = weighted / jnp.transpose(denominator, (2, 0, 1))[..., None]
    return weighted.astype(jnp.bfloat16).reshape(TOKB, -1)


def reference(queries, keys, values, gates, out_weight):
    head_group = HQ // KVH
    causal = jnp.arange(TOKB)[:, None] >= jnp.arange(TOKB)[None, :]
    head_index = jnp.arange(KVH, dtype=jnp.int32)

    def one_sequence(inputs):
        seq_queries, seq_keys, seq_values, seq_gates = inputs
        key_blocks = seq_keys.reshape(NB, TOKB, KVH, HD)
        value_blocks = seq_values.reshape(NB, TOKB, KVH, HD)
        query_blocks = seq_queries.reshape(NB, TOKB, KVH, head_group, HD)

        def one_block(block_index):
            selected = seq_gates[block_index]
            own_keys = jnp.transpose(key_blocks[block_index], (1, 0, 2))
            own_values = jnp.transpose(value_blocks[block_index], (1, 0, 2))
            picked_keys = key_blocks[selected, :, head_index[:, None], :]
            picked_values = value_blocks[selected, :, head_index[:, None], :]
            key_rows = jnp.concatenate([own_keys[:, None], picked_keys], axis=1).reshape(KVH, (1 + PICKS) * TOKB, HD)
            value_rows = jnp.concatenate([own_values[:, None], picked_values], axis=1).reshape(KVH, (1 + PICKS) * TOKB, HD)
            usable = selected < block_index
            pick_allow = jnp.broadcast_to(usable[:, None, :, None], (KVH, TOKB, PICKS, TOKB)).reshape(KVH, TOKB, PICKS * TOKB)
            own_allow = jnp.broadcast_to(causal[None], (KVH, TOKB, TOKB))
            allowed = jnp.concatenate([own_allow, pick_allow], axis=2)
            return attend_rows(query_blocks[block_index], key_rows, value_rows, allowed)

        blocks_out = lax.map(one_block, jnp.arange(NB, dtype=jnp.int32))
        return blocks_out.reshape(L, HQ * HD)

    attended = lax.map(one_sequence, (queries, keys, values, gates))
    share = HQ * HD // N_TP
    features = jnp.transpose(attended.reshape(SEQ * L, N_TP, share), (1, 0, 2))
    weight_parts = out_weight.reshape(N_TP, share, D_OUT)

    def accumulate(summed, inputs):
        feature_part, weight_part = inputs
        partial_value = jnp.dot(feature_part, weight_part, preferred_element_type=jnp.float32).astype(jnp.bfloat16)
        partial_value = lax.optimization_barrier(partial_value)
        return summed + partial_value.astype(jnp.float32), None

    summed, _ = lax.scan(accumulate, jnp.zeros((SEQ * L, D_OUT), jnp.float32), (features, weight_parts))
    return summed.astype(jnp.bfloat16).reshape(SEQ, L, D_OUT)
```

```python
import functools

import jax
import jax.numpy as jnp
from jax import lax
from jax.experimental import pallas as pl
from jax.experimental.pallas import tpu as pltpu
from jax.sharding import PartitionSpec as P

MESH = pl.DeviceIdType.MESH
HD = 128
TOKB = 512
PICKS = 3
TILE = 128
PAIR = 2
FINAL_LAG = 3
LOW = -1e30
VMEM_LIMIT = 60 * 1024 * 1024


def kernel(
    n_ctx, n_tp, q_ref, k_ref, v_ref, gates_ref, w_hbm, out_ref,
    kbuf, vbuf, wbuf, att, part, from_left, from_right, acc,
    local_sem, w_sem, kv_send, kv_recv, rs_send, left_recv, right_recv,
):
    me = lax.axis_index("ctx")
    rank = lax.axis_index("tp")
    blocks = k_ref.shape[0]
    kv_heads = k_ref.shape[2] // HD
    group = q_ref.shape[1] // HD // kv_heads
    tiles = q_ref.shape[0] // TILE
    block_tiles = TOKB // TILE
    width = wbuf.shape[2]
    chips = n_ctx // 2
    chip, core = me // 2, me % 2
    sibling = chip * 2 + (1 - core)
    right = lax.rem(rank + 1, n_tp)
    left = lax.rem(rank + n_tp - 1, n_tp)

    for d in range(n_tp):
        pltpu.make_async_copy(
            w_hbm.at[:, pl.ds(d * width, width)], wbuf.at[d], w_sem.at[d]
        ).start()

    def slot(buf, device):
        return buf.at[pl.ds(device * blocks, blocks)]

    own = []
    for i, (src, buf) in enumerate(((k_ref, kbuf), (v_ref, vbuf))):
        copy = pltpu.make_async_copy(src, slot(buf, me), local_sem.at[i])
        copy.start()
        own.append(copy)

    barrier = pltpu.get_barrier_semaphore()
    for off in range(1, chips):
        peer = lax.rem(chip + off, chips) * 2 + core
        pl.semaphore_signal(barrier, inc=1, device_id={"ctx": peer}, device_id_type=MESH)
    pl.semaphore_signal(barrier, inc=1, device_id={"ctx": sibling}, device_id_type=MESH)

    @pl.when(rank > 0)
    def _():
        pl.semaphore_signal(barrier, inc=1, device_id={"tp": left}, device_id_type=MESH)

    @pl.when(rank < n_tp - 1)
    def _():
        pl.semaphore_signal(barrier, inc=1, device_id={"tp": right}, device_id_type=MESH)

    pl.semaphore_wait(
        barrier, chips + jnp.where(rank > 0, 1, 0) + jnp.where(rank < n_tp - 1, 1, 0)
    )

    def kv_copies(src_k, src_v, source, target, level, off):
        made = []
        for i, (src, buf) in enumerate(((src_k, kbuf), (src_v, vbuf))):
            made.append(
                pltpu.make_async_remote_copy(
                    src_ref=src,
                    dst_ref=slot(buf, source),
                    send_sem=kv_send.at[i, level, off],
                    recv_sem=kv_recv.at[i, source],
                    device_id={"ctx": target},
                    device_id_type=MESH,
                )
            )
        return made

    sent = []
    for off in range(1, chips):
        peer = lax.rem(chip + off, chips) * 2 + core
        for copy in kv_copies(k_ref, v_ref, me, peer, 0, off):
            copy.start()
            sent.append(copy)
    for copy in kv_copies(k_ref, v_ref, me, sibling, 1, 0):
        copy.start()
        sent.append(copy)
    for off in range(1, chips):
        source = lax.rem(chip + chips - off, chips) * 2 + core
        copies = kv_copies(slot(kbuf, source), slot(vbuf, source), source, sibling, 1, off)
        for copy in copies:
            copy.wait_recv()
            copy.start()
            sent.append(copy)
    for off in range(chips):
        source = lax.rem(chip + chips - off, chips) * 2 + (1 - core)
        for copy in kv_copies(slot(kbuf, source), slot(vbuf, source), source, sibling, 1, off):
            copy.wait_recv()
    for copy in own:
        copy.wait()
    for d in range(n_tp):
        pltpu.make_async_copy(
            w_hbm.at[:, pl.ds(d * width, width)], wbuf.at[d], w_sem.at[d]
        ).wait()

    def rs_copy(d, t, rightward):
        return pltpu.make_async_remote_copy(
            src_ref=part.at[d, t],
            dst_ref=(from_left if rightward else from_right).at[d, t],
            send_sem=rs_send.at[d, t],
            recv_sem=(left_recv if rightward else right_recv).at[d, t],
            device_id={"tp": right if rightward else left},
            device_id_type=MESH,
        )

    factor = HD ** (-0.5) * 1.4426950408889634
    pairs = group // PAIR

    def attend(t):
        b = t // block_tiles
        row0 = pl.multiple_of(t * TILE, TILE)
        in_block = (t % block_tiles) * TILE
        own_block = me * blocks + b

        def unit(i, carry):
            e = i // pairs
            lane0 = i * PAIR * HD
            kv_lane = pl.ds(pl.multiple_of(e * HD, HD), HD)
            lanes = [pl.ds(pl.multiple_of(lane0 + h * HD, HD), HD) for h in range(PAIR)]
            q = jnp.concatenate([q_ref[pl.ds(row0, TILE), lane] for lane in lanes], axis=0)
            index, bias = [own_block], [None]
            for j in range(PICKS):
                g = gates_ref[(b * kv_heads + e) * PICKS + j]
                valid = g < own_block
                index.append(jnp.where(valid, g, own_block))
                bias.append(jnp.where(valid, 0.0, LOW).astype(jnp.float32))
            scores = []
            for j in range(PICKS + 1):
                s = lax.dot_general(
                    q, kbuf[index[j], :, kv_lane], (((1,), (1,)), ((), ())),
                    preferred_element_type=jnp.float32,
                )
                if j == 0:
                    row = lax.broadcasted_iota(jnp.int32, s.shape, 0) % TILE + in_block
                    col = lax.broadcasted_iota(jnp.int32, s.shape, 1)
                    s = jnp.where(row >= col, s, LOW)
                else:
                    s = s + bias[j]
                scores.append(s)
            largest = functools.reduce(
                jnp.maximum, [jnp.max(s, axis=1, keepdims=True) for s in scores]
            )
            total, summed = 0.0, 0.0
            for j in range(PICKS + 1):
                raw = jnp.exp2((scores[j] - largest) * factor)
                total = total + jnp.sum(raw, axis=1, keepdims=True)
                summed = summed + jnp.dot(
                    raw.astype(jnp.bfloat16), vbuf[index[j], :, kv_lane],
                    preferred_element_type=jnp.float32,
                )
            result = (summed / total).astype(jnp.bfloat16)
            for h, lane in enumerate(lanes):
                att[:, lane] = result[h * TILE:(h + 1) * TILE]
            return carry

        lax.fori_loop(0, kv_heads * pairs, unit, 0)

    def project(t):
        def chunk(i, carry):
            d = jnp.where(rank < n_tp // 2, n_tp - 1 - i, i)
            part[d, t] = jnp.dot(
                att[...], wbuf[d], preferred_element_type=jnp.float32
            ).astype(jnp.bfloat16)

            @pl.when((rank == 0) & (d > 0))
            def _():
                rs_copy(d, t, True).start()

            @pl.when((rank == n_tp - 1) & (d < n_tp - 1))
            def _():
                rs_copy(d, t, False).start()

            return carry

        lax.fori_loop(0, n_tp, chunk, 0)

    def pass_on(t):
        def go_right(i, carry):
            d = n_tp - 1 - i

            @pl.when((d > rank) & (rank > 0))
            def _():
                copy = rs_copy(d, t, True)
                copy.wait_recv()
                part[d, t] = (
                    part[d, t].astype(jnp.float32) + from_left[d, t].astype(jnp.float32)
                ).astype(jnp.bfloat16)
                copy.start()

            return carry

        def go_left(d, carry):
            @pl.when((d < rank) & (rank < n_tp - 1))
            def _():
                copy = rs_copy(d, t, False)
                copy.wait_recv()
                part[d, t] = (
                    part[d, t].astype(jnp.float32) + from_right[d, t].astype(jnp.float32)
                ).astype(jnp.bfloat16)
                copy.start()

            return carry

        lax.fori_loop(0, n_tp, go_right, 0)
        lax.fori_loop(0, n_tp, go_left, 0)

    def finish(t):
        acc[...] = part[rank, t].astype(jnp.float32)

        @pl.when(rank > 0)
        def _():
            rs_copy(rank, t, True).wait_recv()
            acc[...] += from_left[rank, t].astype(jnp.float32)

        @pl.when(rank < n_tp - 1)
        def _():
            rs_copy(rank, t, False).wait_recv()
            acc[...] += from_right[rank, t].astype(jnp.float32)

        out_ref[pl.ds(pl.multiple_of(t * TILE, TILE), TILE), :] = acc[...].astype(jnp.bfloat16)

    def step(s, carry):
        @pl.when(s < tiles)
        def _():
            attend(s)
            project(s)

        @pl.when((s >= 1) & (s <= tiles))
        def _():
            pass_on(s - 1)

        @pl.when(s >= FINAL_LAG)
        def _():
            finish(s - FINAL_LAG)

        return carry

    lax.fori_loop(0, tiles + FINAL_LAG, step, 0)

    def drain(i, carry):
        d, t = i // tiles, i % tiles

        @pl.when(d != rank)
        def _():
            rs_copy(d, t, True).wait_send()

        return carry

    lax.fori_loop(0, n_tp * tiles, drain, 0)
    for copy in sent:
        copy.wait_send()


def per_device(n_ctx, n_tp, queries, keys, values, gates, out_weight):
    seqs, rows, q_width = queries.shape
    kv_width = keys.shape[2]
    blocks = rows // TOKB
    tiles = rows // TILE
    chips = n_ctx // 2
    depth, features = out_weight.shape
    width = features // n_tp
    vmem = pl.BlockSpec(memory_space=pltpu.VMEM)
    bf16 = jnp.bfloat16
    out = pl.pallas_call(
        functools.partial(kernel, n_ctx, n_tp),
        out_shape=jax.ShapeDtypeStruct((rows, width), bf16),
        in_specs=[
            vmem, vmem, vmem,
            pl.BlockSpec(memory_space=pltpu.SMEM),
            pl.BlockSpec(memory_space=pl.ANY),
        ],
        out_specs=vmem,
        scratch_shapes=[
            pltpu.VMEM((n_ctx * blocks, TOKB, kv_width), bf16),
            pltpu.VMEM((n_ctx * blocks, TOKB, kv_width), bf16),
            pltpu.VMEM((n_tp, depth, width), bf16),
            pltpu.VMEM((TILE, q_width), bf16),
            pltpu.VMEM((n_tp, tiles, TILE, width), bf16),
            pltpu.VMEM((n_tp, tiles, TILE, width), bf16),
            pltpu.VMEM((n_tp, tiles, TILE, width), bf16),
            pltpu.VMEM((TILE, width), jnp.float32),
            pltpu.SemaphoreType.DMA((2,)),
            pltpu.SemaphoreType.DMA((n_tp,)),
            pltpu.SemaphoreType.DMA((2, 2, chips)),
            pltpu.SemaphoreType.DMA((2, n_ctx)),
            pltpu.SemaphoreType.DMA((n_tp, tiles)),
            pltpu.SemaphoreType.DMA((n_tp, tiles)),
            pltpu.SemaphoreType.DMA((n_tp, tiles)),
        ],
        compiler_params=pltpu.CompilerParams(
            collective_id=0, has_side_effects=True, vmem_limit_bytes=VMEM_LIMIT
        ),
        cost_estimate=pl.CostEstimate(
            flops=4 * rows * q_width * (PICKS + 1) * TOKB + 2 * rows * depth * features,
            bytes_accessed=2 * (rows * q_width + 2 * rows * kv_width + depth * features),
            transcendentals=rows * (q_width // HD) * (PICKS + 1) * TOKB,
        ),
    )(
        queries.reshape(rows, q_width),
        keys.reshape(blocks, TOKB, kv_width),
        values.reshape(blocks, TOKB, kv_width),
        gates.reshape(-1),
        out_weight,
    )
    return out.reshape(seqs, rows, width)


def solution(mesh):
    placed = (
        P(None, "ctx", "tp"),
        P(None, "ctx", "tp"),
        P(None, "ctx", "tp"),
        P(None, "ctx", "tp", None),
        P("tp", None),
    )
    return jax.shard_map(
        functools.partial(per_device, mesh.shape["ctx"], mesh.shape["tp"]),
        mesh=mesh, in_specs=placed, out_specs=P(None, "ctx", "tp"), check_vma=False,
    )
```

```python
import functools
import math

import jax
import jax.numpy as jnp
from jax import lax
from jax.experimental import pallas as pl
from jax.experimental.pallas import tpu as pltpu
from jax.sharding import PartitionSpec as P

MESH = pl.DeviceIdType.MESH
HD = 128
TOKB = 512
PICKS = 3
TILE = 128
PAIR = 2
FIRST_FAR = 2
LOW = -1e30
VMEM_LIMIT = 60 * 1024 * 1024


def kernel(
    n_ctx, n_tp, q_ref, k_ref, v_ref, gates_ref, w_hbm, out_ref,
    kbuf, vbuf, wbuf, w_far, att, att_far, part, from_left, from_right, acc,
    local_sem, w_sem, kv_send, kv_recv, rs_send, left_recv, right_recv,
    att_send, att_recv, slice_send, slice_recv, far_send, far_recv, relay_send,
):
    me = lax.axis_index("ctx")
    rank = lax.axis_index("tp")
    blocks = k_ref.shape[0]
    kv_heads = k_ref.shape[2] // HD
    group = q_ref.shape[1] // HD // kv_heads
    tiles = q_ref.shape[0] // TILE
    block_tiles = TOKB // TILE
    width = wbuf.shape[2]
    chips = n_ctx // 2
    chip, core = me // 2, me % 2
    sibling = chip * 2 + (1 - core)
    right = lax.rem(rank + 1, n_tp)
    left = lax.rem(rank + n_tp - 1, n_tp)

    for d in range(n_tp):
        pltpu.make_async_copy(
            w_hbm.at[:, pl.ds(d * width, width)], wbuf.at[d], w_sem.at[d]
        ).start()

    def slot(buf, device):
        return buf.at[pl.ds(device * blocks, blocks)]

    own = []
    for i, (src, buf) in enumerate(((k_ref, kbuf), (v_ref, vbuf))):
        copy = pltpu.make_async_copy(src, slot(buf, me), local_sem.at[i])
        copy.start()
        own.append(copy)

    barrier = pltpu.get_barrier_semaphore()
    for off in range(1, chips):
        peer = lax.rem(chip + off, chips) * 2 + core
        pl.semaphore_signal(barrier, inc=1, device_id={"ctx": peer}, device_id_type=MESH)
    pl.semaphore_signal(barrier, inc=1, device_id={"ctx": sibling}, device_id_type=MESH)

    @pl.when(rank > 0)
    def _():
        pl.semaphore_signal(barrier, inc=1, device_id={"tp": left}, device_id_type=MESH)

    @pl.when(rank < n_tp - 1)
    def _():
        pl.semaphore_signal(barrier, inc=1, device_id={"tp": right}, device_id_type=MESH)

    pl.semaphore_wait(
        barrier, chips + jnp.where(rank > 0, 1, 0) + jnp.where(rank < n_tp - 1, 1, 0)
    )

    def kv_copies(src_k, src_v, source, target, level, off):
        made = []
        for i, (src, buf) in enumerate(((src_k, kbuf), (src_v, vbuf))):
            made.append(
                pltpu.make_async_remote_copy(
                    src_ref=src,
                    dst_ref=slot(buf, source),
                    send_sem=kv_send.at[i, level, off],
                    recv_sem=kv_recv.at[i, source],
                    device_id={"ctx": target},
                    device_id_type=MESH,
                )
            )
        return made

    side = math.isqrt(chips)
    x = chip % side

    def peer_chip(off):
        return lax.rem(chip + off, chips)

    def diagonal(first, second):
        return (first % side != second % side) & (first // side != second // side)

    def start_all(copies):
        for copy in copies:
            copy.start()

    def first_hop(off):
        target = peer_chip(off)
        return kv_copies(k_ref, v_ref, me, target * 2 + core, 0, off)

    for off in range(1, chips):
        target = peer_chip(off)
        copy_k, copy_v = first_hop(off)

        @pl.when(target > chip)
        def _():
            copy_k.start()

        @pl.when((target > chip) & jnp.logical_not(diagonal(chip, target)))
        def _():
            copy_v.start()

    start_all(kv_copies(k_ref, v_ref, me, sibling, 1, 0))

    far_rows = wbuf.shape[1] // n_ctx
    at_end = (rank == 0) | (rank == n_tp - 1)
    helper = (rank == 1) | (rank == n_tp - 2)
    inward = jnp.where(rank == 0, right, left)

    def far_slice(device):
        return w_far.at[:, pl.ds(pl.multiple_of(device * far_rows, far_rows), far_rows)]

    def slice_copy():
        first = jnp.where(rank == 0, 2, 0)
        return pltpu.make_async_remote_copy(
            src_ref=wbuf.at[
                pl.ds(first, n_tp - 2),
                pl.ds(pl.multiple_of(me * far_rows, far_rows), far_rows),
            ],
            dst_ref=far_slice(me),
            send_sem=slice_send,
            recv_sem=slice_recv,
            device_id={"tp": inward},
            device_id_type=MESH,
        )

    def far_copy(source, target, level, off):
        return pltpu.make_async_remote_copy(
            src_ref=far_slice(source),
            dst_ref=far_slice(source),
            send_sem=far_send.at[level, off],
            recv_sem=far_recv.at[source],
            device_id={"ctx": target},
            device_id_type=MESH,
        )

    for d in range(n_tp):
        pltpu.make_async_copy(
            w_hbm.at[:, pl.ds(d * width, width)], wbuf.at[d], w_sem.at[d]
        ).wait()

    @pl.when(at_end)
    def _():
        slice_copy().start()

    def relay_copy(source_chip, column):
        source = source_chip * 2 + core
        return pltpu.make_async_remote_copy(
            src_ref=slot(vbuf, source),
            dst_ref=slot(vbuf, source),
            send_sem=relay_send.at[source_chip, column],
            recv_sem=kv_recv.at[1, source],
            device_id={"ctx": ((chip // side) * side + column) * 2 + core},
            device_id_type=MESH,
        )

    def relays(off, act):
        source_chip = lax.rem(chip + chips - off, chips)
        for column in range(side):
            target = (chip // side) * side + column

            @pl.when(
                (source_chip < chip) & (source_chip % side == x) & (column != x)
                & (source_chip < target)
            )
            def _():
                act(relay_copy(source_chip, column))

    def forward_copies(off):
        source = lax.rem(chip + chips - off, chips) * 2 + core
        return kv_copies(slot(kbuf, source), slot(vbuf, source), source, sibling, 1, off)

    for off in sorted(range(1, chips), key=lambda o: (-(o % side == 0), o)):
        source_chip = lax.rem(chip + chips - off, chips)

        @pl.when(source_chip < chip)
        def _():
            copy_k, copy_v = forward_copies(off)
            copy_v.wait_recv()
            copy_v.start()
            relays(off, lambda copy: copy.start())
            copy_k.wait_recv()
            copy_k.start()

    for off in range(chips):
        source_chip = lax.rem(chip + chips - off, chips)
        source = source_chip * 2 + (1 - core)

        @pl.when(source_chip <= chip)
        def _():
            for copy in kv_copies(slot(kbuf, source), slot(vbuf, source), source, sibling, 1, off):
                copy.wait_recv()

    for copy in own:
        copy.wait()

    @pl.when(helper)
    def _():
        slice_copy().wait_recv()
        for off in range(1, chips):
            far_copy(me, peer_chip(off) * 2 + core, 0, off).start()
        far_copy(me, sibling, 1, 0).start()

    def far_forward():
        for off in range(1, chips):
            source = lax.rem(chip + chips - off, chips) * 2 + core
            copy = far_copy(source, sibling, 1, off)
            copy.wait_recv()
            copy.start()

    def far_ready():
        for off in range(chips):
            source = lax.rem(chip + chips - off, chips) * 2 + (1 - core)
            far_copy(source, sibling, 1, off).wait_recv()

    def att_copy(t):
        return pltpu.make_async_remote_copy(
            src_ref=att.at[t],
            dst_ref=att_far.at[t],
            send_sem=att_send.at[t],
            recv_sem=att_recv.at[t],
            device_id={"tp": inward},
            device_id_type=MESH,
        )

    def rs_copy(d, t, rightward):
        return pltpu.make_async_remote_copy(
            src_ref=part.at[d, t],
            dst_ref=from_left.at[d - 1, t] if rightward else from_right.at[d, t],
            send_sem=rs_send.at[d, t],
            recv_sem=(left_recv if rightward else right_recv).at[d, t],
            device_id={"tp": right if rightward else left},
            device_id_type=MESH,
        )

    factor = HD ** (-0.5) * 1.4426950408889634
    pairs = group // PAIR

    def attend(t):
        b = t // block_tiles
        row0 = pl.multiple_of(t * TILE, TILE)
        in_block = (t % block_tiles) * TILE
        own_block = me * blocks + b

        def unit(i, carry):
            e = i // pairs
            lane0 = i * PAIR * HD
            kv_lane = pl.ds(pl.multiple_of(e * HD, HD), HD)
            lanes = [pl.ds(pl.multiple_of(lane0 + h * HD, HD), HD) for h in range(PAIR)]
            q = jnp.concatenate([q_ref[pl.ds(row0, TILE), lane] for lane in lanes], axis=0)
            index, bias = [own_block], [None]
            for j in range(PICKS):
                g = gates_ref[(b * kv_heads + e) * PICKS + j]
                valid = g < own_block
                index.append(jnp.where(valid, g, own_block))
                bias.append(jnp.where(valid, 0.0, LOW).astype(jnp.float32))
            scores = []
            for j in range(PICKS + 1):
                s = lax.dot_general(
                    q, kbuf[index[j], :, kv_lane], (((1,), (1,)), ((), ())),
                    preferred_element_type=jnp.float32,
                )
                if j == 0:
                    row = lax.broadcasted_iota(jnp.int32, s.shape, 0) % TILE + in_block
                    col = lax.broadcasted_iota(jnp.int32, s.shape, 1)
                    s = jnp.where(row >= col, s, LOW)
                else:
                    s = s + bias[j]
                scores.append(s)
            largest = functools.reduce(
                jnp.maximum, [jnp.max(s, axis=1, keepdims=True) for s in scores]
            )
            total, summed = 0.0, 0.0
            for j in range(PICKS + 1):
                raw = jnp.exp2((scores[j] - largest) * factor)
                total = total + jnp.sum(raw, axis=1, keepdims=True)
                summed = summed + jnp.dot(
                    raw.astype(jnp.bfloat16), vbuf[index[j], :, kv_lane],
                    preferred_element_type=jnp.float32,
                )
            result = (summed / total).astype(jnp.bfloat16)
            for h, lane in enumerate(lanes):
                att[t, :, lane] = result[h * TILE:(h + 1) * TILE]
            return carry

        lax.fori_loop(0, kv_heads * pairs, unit, 0)

    def raw(d, t):
        near = jnp.where(rank == 0, d < 2, jnp.where(rank == n_tp - 1, d > n_tp - 3, True))
        return near | (t < FIRST_FAR)

    def project(t):
        @pl.when(at_end & (t >= FIRST_FAR))
        def _():
            att_copy(t).start()

        def chunk(i, carry):
            d = jnp.where(rank < n_tp // 2, n_tp - 1 - i, i)

            @pl.when(raw(d, t))
            def _():
                part[d, t] = jnp.dot(
                    att[t], wbuf[d], preferred_element_type=jnp.float32
                ).astype(jnp.bfloat16)

                @pl.when((rank == 0) & (d > 0))
                def _():
                    rs_copy(d, t, True).start()

                @pl.when((rank == n_tp - 1) & (d < n_tp - 1))
                def _():
                    rs_copy(d, t, False).start()

            return carry

        lax.fori_loop(0, n_tp, chunk, 0)

    def add(d, t, other):
        part[d, t] = (part[d, t].astype(jnp.float32) + other).astype(jnp.bfloat16)

    def far_dot(j, t):
        return jnp.dot(att_far[t], w_far[j], preferred_element_type=jnp.float32)

    def await_far(t):
        @pl.when(helper & (t >= FIRST_FAR))
        def _():
            att_copy(t).wait_recv()

    def pass_right(t):
        far = t >= FIRST_FAR

        @pl.when(rank == 1)
        def _():
            await_far(t)

        def go_right(i, carry):
            d = n_tp - 1 - i

            @pl.when((d > rank) & (rank > 0))
            def _():
                copy = rs_copy(d, t, True)

                @pl.when((rank == 1) & far)
                def _():
                    add(d, t, far_dot(d - 2, t))

                @pl.when((rank > 1) | jnp.logical_not(far))
                def _():
                    copy.wait_recv()
                    add(d, t, from_left[d - 1, t].astype(jnp.float32))

                copy.start()

            return carry

        lax.fori_loop(0, n_tp, go_right, 0)

    def pass_left(t):
        far = t >= FIRST_FAR

        @pl.when(rank == n_tp - 2)
        def _():
            await_far(t)

        def go_left(d, carry):
            @pl.when((d < rank) & (rank < n_tp - 1))
            def _():
                copy = rs_copy(d, t, False)

                @pl.when((rank == n_tp - 2) & far)
                def _():
                    add(d, t, far_dot(d, t))

                @pl.when((rank < n_tp - 2) | jnp.logical_not(far))
                def _():
                    copy.wait_recv()
                    add(d, t, from_right[d, t].astype(jnp.float32))

                copy.start()

            return carry

        lax.fori_loop(0, n_tp, go_left, 0)

    def finish(t):
        acc[...] = part[rank, t].astype(jnp.float32)

        @pl.when(rank > 0)
        def _():
            rs_copy(rank, t, True).wait_recv()
            acc[...] += from_left[rank - 1, t].astype(jnp.float32)

        @pl.when(rank < n_tp - 1)
        def _():
            rs_copy(rank, t, False).wait_recv()
            acc[...] += from_right[rank, t].astype(jnp.float32)

        out_ref[pl.ds(pl.multiple_of(t * TILE, TILE), TILE), :] = acc[...].astype(jnp.bfloat16)

    def step(s, carry):
        @pl.when(s < tiles)
        def _():
            attend(s)
            project(s)

        @pl.when(helper & (s == FIRST_FAR))
        def _():
            far_forward()

        @pl.when(helper & (s == FIRST_FAR + 1))
        def _():
            far_ready()

        behind_left = s - rank
        behind_right = s - (n_tp - 1 - rank)

        @pl.when((rank > 0) & (behind_left >= 0) & (behind_left < tiles))
        def _():
            pass_right(behind_left)

        @pl.when((rank < n_tp - 1) & (behind_right >= 0) & (behind_right < tiles))
        def _():
            pass_left(behind_right)

        @pl.when(s >= n_tp)
        def _():
            finish(s - n_tp)

        return carry

    lax.fori_loop(0, tiles + n_tp, step, 0)

    def drain(i, carry):
        d, t = i // tiles, i % tiles

        @pl.when((d > rank) & raw(d, t))
        def _():
            rs_copy(d, t, True).wait_send()

        @pl.when((d < rank) & raw(d, t))
        def _():
            rs_copy(d, t, False).wait_send()

        return carry

    lax.fori_loop(0, n_tp * tiles, drain, 0)

    @pl.when(at_end)
    def _():
        slice_copy().wait_send()

        def drain_att(t, carry):
            att_copy(t).wait_send()
            return carry

        lax.fori_loop(FIRST_FAR, tiles, drain_att, 0)

    @pl.when(helper)
    def _():
        for off in range(1, chips):
            far_copy(me, peer_chip(off) * 2 + core, 0, off).wait_send()
        for off in range(chips):
            source = lax.rem(chip + chips - off, chips) * 2 + core
            far_copy(source, sibling, 1, off).wait_send()

    for off in range(1, chips):
        target = peer_chip(off)
        copy_k, copy_v = first_hop(off)

        @pl.when(target > chip)
        def _():
            copy_k.wait_send()

        @pl.when((target > chip) & jnp.logical_not(diagonal(chip, target)))
        def _():
            copy_v.wait_send()

    for copy in kv_copies(k_ref, v_ref, me, sibling, 1, 0):
        copy.wait_send()
    for off in range(1, chips):
        @pl.when(lax.rem(chip + chips - off, chips) < chip)
        def _():
            for copy in forward_copies(off):
                copy.wait_send()

        relays(off, lambda copy: copy.wait_send())


def per_device(n_ctx, n_tp, queries, keys, values, gates, out_weight):
    seqs, rows, q_width = queries.shape
    kv_width = keys.shape[2]
    blocks = rows // TOKB
    tiles = rows // TILE
    chips = n_ctx // 2
    depth, features = out_weight.shape
    width = features // n_tp
    vmem = pl.BlockSpec(memory_space=pltpu.VMEM)
    bf16 = jnp.bfloat16
    out = pl.pallas_call(
        functools.partial(kernel, n_ctx, n_tp),
        out_shape=jax.ShapeDtypeStruct((rows, width), bf16),
        in_specs=[
            vmem, vmem, vmem,
            pl.BlockSpec(memory_space=pltpu.SMEM),
            pl.BlockSpec(memory_space=pl.ANY),
        ],
        out_specs=vmem,
        scratch_shapes=[
            pltpu.VMEM((n_ctx * blocks, TOKB, kv_width), bf16),
            pltpu.VMEM((n_ctx * blocks, TOKB, kv_width), bf16),
            pltpu.VMEM((n_tp, depth, width), bf16),
            pltpu.VMEM((n_tp - 2, depth, width), bf16),
            pltpu.VMEM((tiles, TILE, q_width), bf16),
            pltpu.VMEM((tiles, TILE, q_width), bf16),
            pltpu.VMEM((n_tp, tiles, TILE, width), bf16),
            pltpu.VMEM((n_tp - 1, tiles, TILE, width), bf16),
            pltpu.VMEM((n_tp - 1, tiles, TILE, width), bf16),
            pltpu.VMEM((TILE, width), jnp.float32),
            pltpu.SemaphoreType.DMA((2,)),
            pltpu.SemaphoreType.DMA((n_tp,)),
            pltpu.SemaphoreType.DMA((2, 2, chips)),
            pltpu.SemaphoreType.DMA((2, n_ctx)),
            pltpu.SemaphoreType.DMA((n_tp, tiles)),
            pltpu.SemaphoreType.DMA((n_tp, tiles)),
            pltpu.SemaphoreType.DMA((n_tp, tiles)),
            pltpu.SemaphoreType.DMA((tiles,)),
            pltpu.SemaphoreType.DMA((tiles,)),
            pltpu.SemaphoreType.DMA(()),
            pltpu.SemaphoreType.DMA(()),
            pltpu.SemaphoreType.DMA((2, chips)),
            pltpu.SemaphoreType.DMA((n_ctx,)),
            pltpu.SemaphoreType.DMA((chips, math.isqrt(chips))),
        ],
        compiler_params=pltpu.CompilerParams(
            collective_id=0, has_side_effects=True, vmem_limit_bytes=VMEM_LIMIT
        ),
        cost_estimate=pl.CostEstimate(
            flops=4 * rows * q_width * (PICKS + 1) * TOKB + 2 * rows * depth * features,
            bytes_accessed=2 * (rows * q_width + 2 * rows * kv_width + depth * features),
            transcendentals=rows * (q_width // HD) * (PICKS + 1) * TOKB,
        ),
    )(
        queries.reshape(rows, q_width),
        keys.reshape(blocks, TOKB, kv_width),
        values.reshape(blocks, TOKB, kv_width),
        gates.reshape(-1),
        out_weight,
    )
    return out.reshape(seqs, rows, width)


def solution(mesh):
    placed = (
        P(None, "ctx", "tp"),
        P(None, "ctx", "tp"),
        P(None, "ctx", "tp"),
        P(None, "ctx", "tp", None),
        P("tp", None),
    )
    return jax.shard_map(
        functools.partial(per_device, mesh.shape["ctx"], mesh.shape["tp"]),
        mesh=mesh, in_specs=placed, out_specs=P(None, "ctx", "tp"), check_vma=False,
    )
```
